256 devices in a mesh: shard: 32 (over y, z), rep: 8 (over x, core).
Axes of the slice: x: 4, y: 4, z: 8, core: 2. Of those that a mesh axis runs over, the one named last changes fastest.
Arguments:
- pooled_grad: float32 [65536, 32, 256], P(('rep', 'shard')), may hold values from -0.24 to 0.24
- present_count: int32 [256, 32], P(('rep', 'shard')), may hold values from 64 to 256, as said below
- members: int32 [65536, 32, 8], P('rep', 'shard'), may hold values from 0 to 511
- rep_pos: int32 [8, 32, 512], P('rep', 'shard'), may hold values from 0 to 1023, as said below
- row_ids: int32 [32, 1024], P('shard'), may hold values from 0 to 4095, as said below
- table: float32 [32, 4096, 256], P('shard'), may hold values from -6 to 6
- accum: float32 [32, 4096], P('shard'), may hold values from 0.5 to 20
Outputs:
- new_rows: float32 [32, 1024, 256], P('shard')
- new_accum: float32 [32, 1024], P('shard')
The draws below stay inside these ranges and needn't reach their ends.
Inputs may be any that keep to these rules, and one draw needn't show every extreme that they name: Every row of present_count has the value 256 in some column. `rep_pos`: for each replica group and table the 512 places are distinct. `row_ids`: for each table the 1024 ids are distinct.
All inputs are finite; a program needn't handle non-finite values. Where the reference program divides by a largest or mean magnitude, that divisor is 1e-20 or more.
Results may differ from the reference program's by a relative error of at most 0.00105.
Values may be sent and summed in bfloat16 or wider, within the bound.
No kernel may reach another device: no remote copies, remote signals or barrier semaphores. Data moves between devices by JAX's collectives and lax.ppermute only.
A program may use at most 128 MiB of HBM per device.

```python
import math
import jax
import jax.numpy as jnp
import numpy as np
from jax import lax

E = 256
B_DEV = 256
POOL = 8
TOUCHED = 512
ACTIVE = 1024
ROWS_DEV = 4096
TABLES = 32
GROUPS = 256
BATCH = 65536
N_SHARD = 32
N_REP = 8


def draw_present_count(key, part):
    key = jax.random.fold_in(key, 11)
    first_key, second_key = jax.random.split(key)
    lowest = max(1, B_DEV // 4)
    base = jax.random.randint(first_key, (GROUPS, TABLES), lowest, B_DEV + 1)
    column = jax.random.randint(second_key, (GROUPS,), 0, TABLES)
    columns = jax.lax.broadcasted_iota(jnp.int32, (GROUPS, TABLES), 1)
    return jnp.where(columns == column[:, None], B_DEV, base).astype(jnp.int32)


def draw_rep_pos(key, part):
    key = jax.random.fold_in(key, 12)
    subkeys = jax.random.split(key, N_REP * TABLES)
    picked = jax.vmap(lambda subkey: jax.random.permutation(subkey, ACTIVE)[:TOUCHED])(subkeys)
    return picked.reshape(N_REP, TABLES, TOUCHED).astype(jnp.int32)


def draw_row_ids(key, part):
    key = jax.random.fold_in(key, 13)
    subkeys = jax.random.split(key, TABLES)
    picked = jax.vmap(lambda subkey: jax.random.permutation(subkey, ROWS_DEV)[:ACTIVE])(subkeys)
    return picked.astype(jnp.int32)


def set_ends(entries, key, least, high):
    longest = entries.shape.index(max(entries.shape))
    spots = []
    for shift in (0, 1):
        where = [jax.random.randint(jax.random.fold_in(key, axis), (), 0, length) for axis, length in enumerate(entries.shape)]
        where[longest] = (where[longest] + shift) % entries.shape[longest]
        spots.append(tuple(where))
    return entries.at[spots[0]].set(least).at[spots[1]].set(high)


def levels(key, shape, cuts, least, top_value):
    loudness = 1.0
    for axis_at, shards_of in cuts:
        steps = jax.random.uniform(jax.random.fold_in(jax.random.fold_in(key, 6), axis_at), (shards_of,), jnp.float32, least / len(cuts), top_value / len(cuts))
        loudness = loudness * jnp.repeat(jnp.exp(steps), shape[axis_at] // shards_of).reshape((-1,) + (1,) * (len(shape) - 1 - axis_at))
    return loudness


def rank_table(count, slope):
    weights = [(1 << 20) // math.isqrt(grade ** slope) + 1 for grade in range(1, count + 1)]
    scale = 1 + sum(weights) // (1 << 30)
    return np.cumsum(np.array([max(1, weight // scale) for weight in weights]))


def ranked(own_key, dims, amount, lean):
    grid = rank_table(amount, lean)
    lot = jax.random.randint(jax.random.fold_in(own_key, 1), dims, 0, int(grid[amount - 1]))
    rank = jnp.searchsorted(jnp.asarray(grid, jnp.int32), lot, side="right")
    return jax.random.permutation(jax.random.fold_in(own_key, 2), amount)[rank].astype(jnp.int32)


def noise(own_key, extent, scale, bound, cuts=(), held_as=jnp.bfloat16):
    factor_of = levels(own_key, extent, cuts, -0.22, 0.18) if cuts else 1.0
    values = jax.random.normal(own_key, extent, jnp.float32) * scale * factor_of
    return jnp.minimum(jnp.maximum(values, -bound), bound).astype(held_as)


def setup_inputs(seed: int = 0) -> dict:
    splits = jax.random.split(jax.random.key(seed), 8)
    pooled_grad = noise(splits[0], (BATCH, TABLES, E), 0.03, 0.24, ((0, 256),), jnp.float32)
    present_count = draw_present_count(jax.random.fold_in(splits[7], 71), 0)
    members = set_ends(ranked(splits[2], (BATCH, TABLES, POOL), TOUCHED, 1), jax.random.fold_in(splits[2], 3), 0, TOUCHED - 1).astype(jnp.int32)
    rep_pos = draw_rep_pos(jax.random.fold_in(splits[7], 71), 0)
    row_ids = draw_row_ids(jax.random.fold_in(splits[7], 71), 0)
    table = noise(splits[5], (TABLES, ROWS_DEV, E), 1.0, 6.0, ((0, 32),), jnp.float32)
    accum = jnp.clip(jnp.exp(math.log(20.0) - 3.6888795 * jax.random.uniform(splits[6], (TABLES, ROWS_DEV), jnp.float32) ** levels(splits[6], (TABLES, ROWS_DEV), ((0, 32),), -0.2, 0.2)), 0.5, 20.0)
    return dict(pooled_grad=pooled_grad, present_count=present_count, members=members, rep_pos=rep_pos, row_ids=row_ids, table=table, accum=accum)


LEARN_RATE = 0.5
SCALE_EPS = 1e-06
ADAGRAD_EPS = 1e-08

def reference(pooled_grad, present_count, members, rep_pos, row_ids, table, accum):
    group_bags = N_SHARD * B_DEV
    position = jnp.arange(BATCH, dtype=jnp.int32) % B_DEV

    def one_table(tab):
        grads_tab = lax.dynamic_index_in_dim(pooled_grad, tab, 1, False)
        count_tab = lax.dynamic_index_in_dim(present_count, tab, 1, False)
        present = (position < jnp.repeat(count_tab, B_DEV, total_repeat_length=BATCH)).astype(jnp.float32)
        grads_tab = grads_tab * present[:, None]
        member_tab = lax.dynamic_index_in_dim(members, tab, 1, False).reshape(N_REP, group_bags * POOL)
        place_tab = lax.dynamic_index_in_dim(rep_pos, tab, 1, False)

        def one_rep(group):
            bag_rows = lax.dynamic_slice_in_dim(grads_tab, group * group_bags, group_bags, 0)
            spread = jnp.repeat(bag_rows, POOL, axis=0)
            row_grads = jax.ops.segment_sum(spread, member_tab[group], num_segments=TOUCHED)
            row_scale = lax.optimization_barrier(jnp.max(jnp.abs(row_grads), axis=1)) + SCALE_EPS
            quantized = (row_grads / row_scale[:, None]).astype(jnp.bfloat16)
            restored = quantized.astype(jnp.float32) * row_scale[:, None]
            return jnp.zeros((ACTIVE, E), jnp.float32).at[place_tab[group]].set(restored)
        dense_rows = lax.map(one_rep, jnp.arange(N_REP, dtype=jnp.int32))
        summed = lax.optimization_barrier(jnp.sum(dense_rows, axis=0))
        row_index = lax.dynamic_index_in_dim(row_ids, tab, 0, False)
        old_rows = jnp.take(lax.dynamic_index_in_dim(table, tab, 0, False), row_index, axis=0)
        old_state = jnp.take(lax.dynamic_index_in_dim(accum, tab, 0, False), row_index, axis=0)
        new_state = old_state + lax.optimization_barrier(jnp.mean(summed * summed, axis=1))
        updated = old_rows - LEARN_RATE * summed / (jnp.sqrt(new_state)[:, None] + ADAGRAD_EPS)
        return (updated, new_state)
    new_rows, new_accum = lax.map(one_table, jnp.arange(TABLES, dtype=jnp.int32))
    return (new_rows, new_accum)
```

```python
import functools

import jax
import jax.numpy as jnp
from jax import lax
from jax.experimental import pallas as pl
from jax.experimental.pallas import tpu as pltpu
from jax.sharding import Mesh
from jax.sharding import PartitionSpec as P

LEARN_RATE = 0.5
ADAGRAD_EPS = 1e-08
PLANE = ("y", "x", "core")
REP = ("x", "core")
MIB = 1 << 20


def mask_kernel(samples, count_ref, left_ref, right_ref, out_ref):
    tables = out_ref.shape[0]
    first = pl.program_id(0) * samples
    position = lax.broadcasted_iota(jnp.int32, (samples, 128), 0) + first
    for table in range(tables):
        present = position < count_ref[0, table]
        for side, grad_ref in enumerate((left_ref, right_ref)):
            rows = grad_ref[pl.ds(table, samples, stride=tables), :]
            kept = jnp.where(present, rows, 0.0)
            out_ref[table, :, pl.ds(side * 128, 128)] = kept.astype(jnp.bfloat16)


def masked_by_table(pooled_grad, present_count):
    batch, tables, width = pooled_grad.shape
    samples = 32
    rows = pooled_grad.reshape(batch * tables, width)
    return pl.pallas_call(
        functools.partial(mask_kernel, samples),
        grid=(batch // samples,),
        out_shape=jax.ShapeDtypeStruct((tables, batch, width), jnp.bfloat16),
        in_specs=[
            pl.BlockSpec(memory_space=pltpu.SMEM),
            pl.BlockSpec((samples * tables, 128), lambda i: (i, 0)),
            pl.BlockSpec((samples * tables, 128), lambda i: (i, 1)),
        ],
        out_specs=pl.BlockSpec((tables, samples, width), lambda i: (0, i, 0)),
        compiler_params=pltpu.CompilerParams(vmem_limit_bytes=16 * MIB),
        cost_estimate=pl.CostEstimate(flops=batch * tables * width, bytes_accessed=batch * tables * width * 6, transcendentals=0),
        name="mask",
    )(present_count, rows, rows)


def place_kernel(members_ref, pos_ref, out_ref):
    n_z, slots, wide = out_ref.shape
    n_y = members_ref.shape[1] // (n_z * 256)
    parts = [jnp.broadcast_to(pos_ref[:, pl.ds(128 * k, 128)], (slots, 128)) for k in range(4)]
    for y in range(n_y):
        for z in range(n_z):
            for half in range(2):
                member = members_ref[:, pl.ds((y * n_z + z) * 256 + half * 128, 128)]
                low, high = member & 127, member >> 7
                found = jnp.take_along_axis(parts[0], low, axis=1)
                for k in range(1, 4):
                    found = jnp.where(high == k, jnp.take_along_axis(parts[k], low, axis=1), found)
                out_ref[z, :, pl.ds(y * 256 + half * 128, 128)] = found


def places_of(members, rep_pos, n_z):
    batch, slots = members.shape
    return pl.pallas_call(
        place_kernel,
        out_shape=jax.ShapeDtypeStruct((n_z, slots, batch // n_z), jnp.int32),
        compiler_params=pltpu.CompilerParams(vmem_limit_bytes=16 * MIB),
        cost_estimate=pl.CostEstimate(flops=batch * slots * 8, bytes_accessed=batch * slots * 8, transcendentals=0),
        name="places",
    )(members.T, rep_pos)


def count_kernel(place_ref, out_ref):
    slots, samples = place_ref.shape[1:]
    place = place_ref[0].astype(jnp.int32)
    high, low = place >> 5, place & 31
    row = lax.broadcasted_iota(jnp.int32, (32, samples), 0).astype(jnp.bfloat16)
    for block in range(out_ref.shape[0] // 32):
        wanted = jnp.where(high == block, low, -1).astype(jnp.bfloat16)
        total = jnp.zeros((32, samples), jnp.bfloat16)
        for slot in range(slots):
            here = jnp.broadcast_to(wanted[slot : slot + 1], (32, samples)) == row
            total = total + jnp.where(here, jnp.bfloat16(1), jnp.bfloat16(0))
        out_ref[pl.ds(block * 32, 32), :] = total


def counts_of(places, active):
    reps, slots, wide = places.shape
    n_y = wide // 256
    return pl.pallas_call(
        count_kernel,
        grid=(n_y, reps),
        out_shape=jax.ShapeDtypeStruct((active, n_y * reps * 256), jnp.bfloat16),
        in_specs=[pl.BlockSpec((1, slots, 256), lambda y, r: (r, 0, y))],
        out_specs=pl.BlockSpec((active, 256), lambda y, r: (0, y * reps + r)),
        compiler_params=pltpu.CompilerParams(vmem_limit_bytes=16 * MIB),
        cost_estimate=pl.CostEstimate(flops=active * wide * reps * slots * 3, bytes_accessed=active * wide * reps * 2, transcendentals=0),
        name="counts",
    )(places)


def local(n_z, n_rep, pooled_grad, present_count, members, rep_pos, row_ids, table, accum):
    active, width = row_ids.shape[1], pooled_grad.shape[2]
    swap = [(z * n_rep + q, q * n_z + z) for z in range(n_z) for q in range(n_rep)]

    places = places_of(members[:, 0, :], rep_pos[0], n_z).astype(jnp.int16)
    places = lax.ppermute(places, ("z",) + REP, swap)
    places = lax.all_to_all(places, "z", split_axis=0, concat_axis=0, tiled=True)
    counts = counts_of(places.astype(jnp.int32), active)

    masked = masked_by_table(pooled_grad, present_count)
    arrived = lax.all_to_all(masked, PLANE, split_axis=0, concat_axis=0, tiled=True)
    partial = jnp.dot(counts, arrived.reshape(-1, width), preferred_element_type=jnp.float32)

    chunks = partial.astype(jnp.bfloat16).reshape(n_z, active // n_z, width)
    chunks = lax.all_to_all(chunks, "z", split_axis=0, concat_axis=0, tiled=True)
    part = jnp.sum(chunks.astype(jnp.float32), axis=0).astype(jnp.bfloat16)
    part = lax.ppermute(part, ("z",) + REP, swap)
    summed = lax.all_gather(part, REP, axis=0, tiled=True).astype(jnp.float32)

    old_rows = jnp.take(table[0], row_ids[0], axis=0)
    old_state = jnp.take(accum[0], row_ids[0], axis=0)
    new_state = old_state + jnp.mean(summed * summed, axis=1)
    updated = old_rows - LEARN_RATE * summed / (jnp.sqrt(new_state)[:, None] + ADAGRAD_EPS)
    return (updated[None], new_state[None])


def solution(mesh):
    n_y, n_z, n_x, n_core = 4, 8, 4, 2
    grid = Mesh(mesh.devices.reshape(n_y, n_z, n_x, n_core), ("y", "z", "x", "core"))
    shard = ("y", "z")
    in_specs = (
        P(REP + shard, None, None),
        P(REP + shard, None),
        P(REP, shard, None),
        P(REP, shard, None),
        P(shard, None),
        P(shard, None, None),
        P(shard, None),
    )
    out_specs = (P(shard, None, None), P(shard, None))
    return jax.shard_map(
        functools.partial(local, n_z, n_x * n_core),
        mesh=grid,
        in_specs=in_specs,
        out_specs=out_specs,
        check_vma=False,
    )
```

```python
import functools

import jax
import jax.numpy as jnp
from jax import lax
from jax.experimental import pallas as pl
from jax.experimental.pallas import tpu as pltpu
from jax.sharding import Mesh
from jax.sharding import PartitionSpec as P

LEARN_RATE = 0.5
ADAGRAD_EPS = 1e-08
REP = ("x", "core")
MIB = 1 << 20


def mask_kernel(n_z, count_ref, grad_ref, out_ref):
    tables, samples, width = out_ref.shape
    n_y = tables // n_z
    first = pl.program_id(0) * samples
    to = lax.broadcasted_iota(jnp.int32, (256, 256), 0)
    source = lax.broadcasted_iota(jnp.int32, (256, 256), 1)
    permute = ((source % 16) * 16 + source // 16 == to).astype(jnp.bfloat16)
    position = lax.broadcasted_iota(jnp.int32, (16, width), 0) + first
    for sample in range(0, samples, 16):
        for table in range(0, tables, 16):
            rows = grad_ref[sample : sample + 16, table : table + 16, :].reshape(256, width)
            moved = jnp.dot(permute, rows.astype(jnp.bfloat16), preferred_element_type=jnp.float32)
            for j in range(16):
                present = position + sample < count_ref[0, table + j]
                kept = jnp.where(present, moved[j * 16 : j * 16 + 16], 0.0)
                place = (table + j) % n_z * n_y + (table + j) // n_z
                out_ref[place, sample : sample + 16, :] = kept.astype(jnp.bfloat16)


def masked_by_table(n_z, pooled_grad, present_count):
    batch, tables, width = pooled_grad.shape
    samples = 128
    return pl.pallas_call(
        functools.partial(mask_kernel, n_z),
        grid=(batch // samples,),
        out_shape=jax.ShapeDtypeStruct((tables, batch, width), jnp.bfloat16),
        in_specs=[
            pl.BlockSpec(memory_space=pltpu.SMEM),
            pl.BlockSpec((samples, tables, width), lambda i: (i, 0, 0)),
        ],
        out_specs=pl.BlockSpec((tables, samples, width), lambda i: (0, i, 0)),
        compiler_params=pltpu.CompilerParams(vmem_limit_bytes=56 * MIB),
        cost_estimate=pl.CostEstimate(flops=batch * tables * width, bytes_accessed=batch * tables * width * 6, transcendentals=0),
        name="mask",
    )(present_count, pooled_grad)


def lists_kernel(members_ref, pos_ref, out_ref):
    n_z, wide = out_ref.shape[0] - 1, out_ref.shape[2]
    n_y, touched = wide // 256, pos_ref.shape[1]
    for y in range(n_y):
        for z in range(n_z):
            out_ref[z, :, pl.ds(y * 256, 256)] = members_ref[:, pl.ds((y * n_z + z) * 256, 256)]
    out_ref[n_z] = jnp.zeros(out_ref.shape[1:], jnp.int32)
    out_ref[n_z, pl.ds(0, 1), pl.ds(0, touched)] = pos_ref[...]


def lists_of(members, rep_pos, n_z):
    batch, slots = members.shape
    return pl.pallas_call(
        lists_kernel,
        out_shape=jax.ShapeDtypeStruct((n_z + 1, slots, batch // n_z), jnp.int32),
        compiler_params=pltpu.CompilerParams(vmem_limit_bytes=8 * MIB),
        cost_estimate=pl.CostEstimate(flops=batch * slots, bytes_accessed=batch * slots * 8, transcendentals=0),
        name="lists",
    )(members.T, rep_pos)


def one_hot_rows(values, row):
    return jnp.where(jnp.broadcast_to(values, row.shape) == row, jnp.bfloat16(1), jnp.bfloat16(0))


def count_kernel(member_ref, out_ref):
    slots, samples = member_ref.shape[1:]
    rows = 32
    base = lax.broadcasted_iota(jnp.int32, (rows, 128), 0).astype(jnp.bfloat16)

    def lanes(i, carry):
        at = pl.ds(pl.multiple_of(i * 128, 128), 128)
        member = member_ref[0, :, at]
        high, low = member >> 8, member & 255
        for block in range(out_ref.shape[1] // 256):
            wanted = jnp.where(high == block, low, -1).astype(jnp.bfloat16)
            for first in range(0, 256, rows):
                row = base + jnp.bfloat16(first)
                total = one_hot_rows(wanted[0:1], row)
                for s in range(1, slots):
                    total = total + one_hot_rows(wanted[s : s + 1], row)
                out_ref[0, pl.ds(block * 256 + first, rows), at] = total
        return carry

    lax.fori_loop(0, samples // 128, lanes, 0)


def counts_of(members, touched):
    reps, slots, wide = members.shape
    return pl.pallas_call(
        count_kernel,
        grid=(reps,),
        in_specs=[pl.BlockSpec((1, slots, wide), lambda r: (r, 0, 0))],
        out_specs=pl.BlockSpec((1, touched, wide), lambda r: (r, 0, 0)),
        out_shape=jax.ShapeDtypeStruct((reps, touched, wide), jnp.bfloat16),
        compiler_params=pltpu.CompilerParams(vmem_limit_bytes=56 * MIB),
        cost_estimate=pl.CostEstimate(flops=touched * wide * reps * slots * 3, bytes_accessed=touched * wide * reps * 2, transcendentals=0),
        name="counts",
    )(members)


AHEAD = 3


def plane_kernel(count_hbm, bags_hbm, pos_ref, out_ref, count_buf, bags_buf, place_buf, grad_buf, total_ref, count_sem, bags_sem):
    reps, touched, samples = count_hbm.shape
    active = out_ref.shape[0]
    row = lax.broadcasted_iota(jnp.int32, (256, 128), 0).astype(jnp.bfloat16)

    def copies(rep):
        slot = rep % AHEAD
        bags = bags_hbm.at[pl.ds(rep * samples, samples), :]
        return (
            pltpu.make_async_copy(count_hbm.at[rep], count_buf.at[slot], count_sem.at[slot]),
            pltpu.make_async_copy(bags, bags_buf.at[slot], bags_sem.at[slot]),
        )

    for rep in range(AHEAD - 1):
        for copy in copies(rep):
            copy.start()
    for rep in range(reps):
        if rep + AHEAD - 1 < reps:
            for copy in copies(rep + AHEAD - 1):
                copy.start()
        first = rep % 2 * touched
        for lane in range(0, touched, 128):
            pos = pos_ref[rep : rep + 1, lane : lane + 128]
            for block in range(active // 256):
                wanted = jnp.where((pos >> 8) == block, pos & 255, -1).astype(jnp.bfloat16)
                place_buf[pl.ds(block * 256, 256), pl.ds(first + lane, 128)] = one_hot_rows(wanted, row)
        for copy in copies(rep):
            copy.wait()
        slot = rep % AHEAD
        grads = jnp.dot(count_buf[slot], bags_buf[slot], preferred_element_type=jnp.float32)
        grad_buf[pl.ds(first, touched), :] = grads.astype(jnp.bfloat16)
        if rep % 2:
            sums = jnp.dot(place_buf[...], grad_buf[...], preferred_element_type=jnp.float32)
            if rep == 1:
                total_ref[...] = sums
            elif rep < reps - 1:
                total_ref[...] += sums
            else:
                out_ref[...] = (total_ref[...] + sums).astype(jnp.bfloat16)


def plane_sum(counts, bags, pos, active):
    reps, touched, samples = counts.shape
    width = bags.shape[1]
    return pl.pallas_call(
        plane_kernel,
        out_shape=jax.ShapeDtypeStruct((active, width), jnp.bfloat16),
        in_specs=[
            pl.BlockSpec(memory_space=pl.ANY),
            pl.BlockSpec(memory_space=pl.ANY),
            pl.BlockSpec(memory_space=pltpu.VMEM),
        ],
        out_specs=pl.BlockSpec(memory_space=pltpu.VMEM),
        scratch_shapes=[
            pltpu.VMEM((AHEAD, touched, samples), jnp.bfloat16),
            pltpu.VMEM((AHEAD, samples, width), jnp.bfloat16),
            pltpu.VMEM((active, 2 * touched), jnp.bfloat16),
            pltpu.VMEM((2 * touched, width), jnp.bfloat16),
            pltpu.VMEM((active, width), jnp.float32),
            pltpu.SemaphoreType.DMA((AHEAD,)),
            pltpu.SemaphoreType.DMA((AHEAD,)),
        ],
        compiler_params=pltpu.CompilerParams(vmem_limit_bytes=56 * MIB),
        cost_estimate=pl.CostEstimate(
            flops=2 * reps * touched * (samples + active) * width,
            bytes_accessed=reps * samples * (touched + width) * 2,
            transcendentals=0,
        ),
        name="plane_sum",
    )(counts, bags, pos)


def local(n_z, n_rep, pooled_grad, present_count, members, rep_pos, row_ids, table, accum):
    active, width = row_ids.shape[1], pooled_grad.shape[2]
    swap = [(z * n_rep + q, q * n_z + z) for z in range(n_z) for q in range(n_rep)]

    lists = lists_of(members[:, 0, :], rep_pos[0], n_z).astype(jnp.int16)
    lists = lax.ppermute(lists, ("z",) + REP, swap)
    lists = lax.all_gather(lists, "z", axis=0, tiled=False)
    here = lax.dynamic_index_in_dim(lists, lax.axis_index("z"), 1, False).astype(jnp.int32)
    touched = rep_pos.shape[2]
    pos = lists[:, n_z, 0, :touched].astype(jnp.int32)

    masked = masked_by_table(n_z, pooled_grad, present_count)
    arrived = lax.all_to_all(masked, REP + ("y",), split_axis=0, concat_axis=0, tiled=True)

    counts = counts_of(here, touched)
    partial = plane_sum(counts, arrived.reshape(-1, width), pos, active)

    chunks = partial.reshape(n_z, active // n_z, width)
    chunks = lax.all_to_all(chunks, "z", split_axis=0, concat_axis=0, tiled=True)
    old_rows = jnp.take(table[0], row_ids[0], axis=0)
    old_state = jnp.take(accum[0], row_ids[0], axis=0)
    chunks, old_rows, old_state = lax.optimization_barrier((chunks, old_rows, old_state))
    part = jnp.sum(chunks.astype(jnp.float32), axis=0).astype(jnp.bfloat16)
    part = lax.ppermute(part, ("z",) + REP, swap)
    summed = lax.all_gather(part, REP, axis=0, tiled=True).astype(jnp.float32)

    new_state = old_state + jnp.mean(summed * summed, axis=1)
    updated = old_rows - LEARN_RATE * summed / (jnp.sqrt(new_state)[:, None] + ADAGRAD_EPS)
    return (updated[None], new_state[None])


def solution(mesh):
    n_y, n_z, n_x, n_core = 4, 8, 4, 2
    grid = Mesh(mesh.devices.reshape(n_y, n_z, n_x, n_core), ("y", "z", "x", "core"))
    shard = ("y", "z")
    in_specs = (
        P(REP + shard, None, None),
        P(REP + shard, None),
        P(REP, shard, None),
        P(REP, shard, None),
        P(shard, None),
        P(shard, None, None),
        P(shard, None),
    )
    out_specs = (P(shard, None, None), P(shard, None))
    return jax.shard_map(
        functools.partial(local, n_z, n_x * n_core),
        mesh=grid,
        in_specs=in_specs,
        out_specs=out_specs,
        check_vma=False,
    )
```

```python
import functools

import jax
import jax.numpy as jnp
from jax import lax
from jax.experimental import pallas as pl
from jax.experimental.pallas import tpu as pltpu
from jax.sharding import Mesh
from jax.sharding import PartitionSpec as P

LEARN_RATE = 0.5
ADAGRAD_EPS = 1e-08
REP = ("x", "core")
MIB = 1 << 20


def mask_kernel(n_z, count_ref, grad_ref, out_ref):
    tables, samples, width = out_ref.shape
    n_y = tables // n_z
    first = pl.program_id(0) * samples
    to = lax.broadcasted_iota(jnp.int32, (256, 256), 0)
    source = lax.broadcasted_iota(jnp.int32, (256, 256), 1)
    permute = ((source % 16) * 16 + source // 16 == to).astype(jnp.bfloat16)
    position = lax.broadcasted_iota(jnp.int32, (16, width), 0) + first
    for sample in range(0, samples, 16):
        for table in range(0, tables, 16):
            rows = grad_ref[sample : sample + 16, table : table + 16, :].reshape(256, width)
            moved = jnp.dot(permute, rows.astype(jnp.bfloat16), preferred_element_type=jnp.float32)
            for j in range(16):
                present = position + sample < count_ref[0, table + j]
                kept = jnp.where(present, moved[j * 16 : j * 16 + 16], 0.0)
                place = (table + j) % n_z * n_y + (table + j) // n_z
                out_ref[place, sample : sample + 16, :] = kept.astype(jnp.bfloat16)


def masked_by_table(n_z, pooled_grad, present_count):
    batch, tables, width = pooled_grad.shape
    samples = 128
    return pl.pallas_call(
        functools.partial(mask_kernel, n_z),
        grid=(batch // samples,),
        out_shape=jax.ShapeDtypeStruct((tables, batch, width), jnp.bfloat16),
        in_specs=[
            pl.BlockSpec(memory_space=pltpu.SMEM),
            pl.BlockSpec((samples, tables, width), lambda i: (i, 0, 0)),
        ],
        out_specs=pl.BlockSpec((tables, samples, width), lambda i: (0, i, 0)),
        compiler_params=pltpu.CompilerParams(vmem_limit_bytes=56 * MIB),
        cost_estimate=pl.CostEstimate(flops=batch * tables * width, bytes_accessed=batch * tables * width * 6, transcendentals=0),
        name="mask",
    )(present_count, pooled_grad)


def place_kernel(z_ref, members_ref, pos_ref, out_ref):
    n_z, slots, wide = out_ref.shape
    n_y = wide // 256
    parts = [jnp.broadcast_to(pos_ref[:, pl.ds(128 * k, 128)], (slots, 128)) for k in range(pos_ref.shape[1] // 128)]
    for j in range(n_z):
        z = lax.bitwise_xor(z_ref[0], j)
        for y in range(n_y):
            for half in range(2):
                start = pl.multiple_of((y * n_z + z) * 256 + half * 128, 128)
                member = members_ref[:, pl.ds(start, 128)]
                low, high = member & 127, member >> 7
                found = jnp.take_along_axis(parts[0], low, axis=1)
                for k in range(1, len(parts)):
                    found = jnp.where(high == k, jnp.take_along_axis(parts[k], low, axis=1), found)
                out_ref[j, :, pl.ds(y * 256 + half * 128, 128)] = found


def places_of(members, rep_pos, z, n_z):
    batch, slots = members.shape
    return pl.pallas_call(
        place_kernel,
        out_shape=jax.ShapeDtypeStruct((n_z, slots, batch // n_z), jnp.int32),
        in_specs=[
            pl.BlockSpec(memory_space=pltpu.SMEM),
            pl.BlockSpec(memory_space=pltpu.VMEM),
            pl.BlockSpec(memory_space=pltpu.VMEM),
        ],
        compiler_params=pltpu.CompilerParams(vmem_limit_bytes=8 * MIB),
        cost_estimate=pl.CostEstimate(flops=batch * slots * 8, bytes_accessed=batch * slots * 8, transcendentals=0),
        name="places",
    )(z, members.T, rep_pos)


def turn(v):
    return (v * 2) ^ (v // 4 * 11)


def from_turn(v):
    return (v ^ ((v & 1) * 11)) >> 1


def exchange_over_z(places):
    n_z = places.shape[0]
    places = places.reshape((2, 2, 2) + places.shape[1:])
    for axis, bit in enumerate((4, 2, 1)):
        stay = lax.index_in_dim(places, 0, axis, False)
        go = lax.index_in_dim(places, 1, axis, False)
        come = lax.ppermute(go, "z", [(z, z ^ bit) for z in range(n_z)])
        places = jnp.stack([stay, come], axis)
    return places.reshape((n_z,) + places.shape[3:])


def gather_over_rep(part, n_x):
    x = lax.axis_index("x")
    place = (lax.broadcasted_iota(jnp.int32, (n_x, 1, 1), 0) - x + n_x) % n_x
    rows = part[None]
    for step in range(1, n_x):
        come = lax.ppermute(part, "x", [(a, (a - step) % n_x) for a in range(n_x)])
        rows = jnp.where(place == step, come[None], rows)
    return lax.all_gather(rows, "core", axis=1, tiled=False).reshape(-1, part.shape[1])


def one_hot_rows(values, row):
    return jnp.where(jnp.broadcast_to(values, row.shape) == row, jnp.bfloat16(1), jnp.bfloat16(0))


def count_kernel(place_ref, out_ref):
    slots, samples = place_ref.shape[1:]
    rows = 32
    base = lax.broadcasted_iota(jnp.int32, (rows, 128), 0).astype(jnp.bfloat16)

    def lanes(i, carry):
        at = pl.ds(pl.multiple_of(i * 128, 128), 128)
        place = place_ref[0, :, at]
        high, low = place >> 8, place & 255
        for block in range(out_ref.shape[1] // 256):
            wanted = jnp.where(high == block, low, -1).astype(jnp.bfloat16)
            for first in range(0, 256, rows):
                row = base + jnp.bfloat16(first)
                total = one_hot_rows(wanted[0:1], row)
                for s in range(1, slots):
                    total = total + one_hot_rows(wanted[s : s + 1], row)
                out_ref[0, pl.ds(block * 256 + first, rows), at] = total
        return carry

    lax.fori_loop(0, samples // 128, lanes, 0)


def counts_of(places, active):
    reps, slots, wide = places.shape
    return pl.pallas_call(
        count_kernel,
        grid=(reps,),
        in_specs=[pl.BlockSpec((1, slots, wide), lambda j: (j, 0, 0))],
        out_specs=pl.BlockSpec((1, active, wide), lambda j: (j, 0, 0)),
        out_shape=jax.ShapeDtypeStruct((reps, active, wide), jnp.bfloat16),
        compiler_params=pltpu.CompilerParams(vmem_limit_bytes=56 * MIB),
        cost_estimate=pl.CostEstimate(flops=active * wide * reps * slots * 3, bytes_accessed=active * wide * reps * 2, transcendentals=0),
        name="counts",
    )(places)


AHEAD = 4


def plane_kernel(z_ref, rep_ref, count_hbm, bags_hbm, out_ref, count_buf, bags_buf, total_ref, count_sem, bags_sem):
    reps, _, samples = count_hbm.shape

    def copies(j):
        slot = lax.rem(j, AHEAD)
        group = rep_ref[0] ^ from_turn(z_ref[0] ^ j ^ rep_ref[0])
        start = pl.multiple_of(group * samples, samples)
        return (
            pltpu.make_async_copy(count_hbm.at[j], count_buf.at[slot], count_sem.at[slot]),
            pltpu.make_async_copy(bags_hbm.at[pl.ds(start, samples), :], bags_buf.at[slot], bags_sem.at[slot]),
        )

    for j in range(AHEAD - 1):
        for copy in copies(jnp.int32(j)):
            copy.start()
    total_ref[...] = jnp.zeros_like(total_ref)

    def step(j, carry):
        @pl.when(j + AHEAD - 1 < reps)
        def _():
            for copy in copies(j + AHEAD - 1):
                copy.start()

        for copy in copies(j):
            copy.wait()
        slot = lax.rem(j, AHEAD)
        total_ref[...] += jnp.dot(count_buf[slot], bags_buf[slot], preferred_element_type=jnp.float32)
        return carry

    lax.fori_loop(0, reps, step, 0)
    out_ref[...] = total_ref[...].astype(jnp.bfloat16)


def plane_sum(z, rep, counts, bags):
    reps, active, samples = counts.shape
    width = bags.shape[1]
    return pl.pallas_call(
        plane_kernel,
        out_shape=jax.ShapeDtypeStruct((active, width), jnp.bfloat16),
        in_specs=[
            pl.BlockSpec(memory_space=pltpu.SMEM),
            pl.BlockSpec(memory_space=pltpu.SMEM),
            pl.BlockSpec(memory_space=pl.ANY),
            pl.BlockSpec(memory_space=pl.ANY),
        ],
        out_specs=pl.BlockSpec(memory_space=pltpu.VMEM),
        scratch_shapes=[
            pltpu.VMEM((AHEAD, active, samples), jnp.bfloat16),
            pltpu.VMEM((AHEAD, samples, width), jnp.bfloat16),
            pltpu.VMEM((active, width), jnp.float32),
            pltpu.SemaphoreType.DMA((AHEAD,)),
            pltpu.SemaphoreType.DMA((AHEAD,)),
        ],
        compiler_params=pltpu.CompilerParams(vmem_limit_bytes=56 * MIB),
        cost_estimate=pl.CostEstimate(
            flops=2 * reps * active * samples * width,
            bytes_accessed=reps * samples * (active + width) * 2,
            transcendentals=0,
        ),
        name="plane_sum",
    )(z, rep, counts, bags)


def local(n_z, n_rep, pooled_grad, present_count, members, rep_pos, row_ids, table, accum):
    active, width = row_ids.shape[1], pooled_grad.shape[2]
    swap = [(z * n_rep + q, q * n_z + z) for z in range(n_z) for q in range(n_rep)]

    z, rep = lax.axis_index("z"), lax.axis_index(REP)
    spread = [(a * n_rep + r, (a ^ turn(r ^ a)) * n_rep + a) for a in range(n_z) for r in range(n_rep)]
    plane = z ^ turn(z ^ rep)
    places = places_of(members[:, 0, :], rep_pos[0], plane.reshape(1), n_z).astype(jnp.int16)
    places = lax.ppermute(places, ("z",) + REP, spread)
    places = exchange_over_z(places).astype(jnp.int32)

    masked = masked_by_table(n_z, pooled_grad, present_count)
    arrived = lax.all_to_all(masked, REP + ("y",), split_axis=0, concat_axis=0, tiled=True)

    counts = counts_of(places, active)
    partial = plane_sum(z.reshape(1), rep.reshape(1), counts, arrived.reshape(-1, width))

    chunks = partial.reshape(n_z, active // n_z, width)
    chunks = lax.all_to_all(chunks, "z", split_axis=0, concat_axis=0, tiled=True)
    old_rows = jnp.take(table[0], row_ids[0], axis=0)
    old_state = jnp.take(accum[0], row_ids[0], axis=0)
    chunks, old_rows, old_state = lax.optimization_barrier((chunks, old_rows, old_state))
    part = jnp.sum(chunks.astype(jnp.float32), axis=0).astype(jnp.bfloat16)
    part = lax.ppermute(part, ("z",) + REP, swap)
    summed = gather_over_rep(part, n_rep // 2).astype(jnp.float32)

    new_state = old_state + jnp.mean(summed * summed, axis=1)
    updated = old_rows - LEARN_RATE * summed / (jnp.sqrt(new_state)[:, None] + ADAGRAD_EPS)
    return (updated[None], new_state[None])


def solution(mesh):
    n_y, n_z, n_x, n_core = 4, 8, 4, 2
    grid = Mesh(mesh.devices.reshape(n_y, n_z, n_x, n_core), ("y", "z", "x", "core"))
    shard = ("y", "z")
    in_specs = (
        P(REP + shard, None, None),
        P(REP + shard, None),
        P(REP, shard, None),
        P(REP, shard, None),
        P(shard, None),
        P(shard, None, None),
        P(shard, None),
    )
    out_specs = (P(shard, None, None), P(shard, None))
    return jax.shard_map(
        functools.partial(local, n_z, n_x * n_core),
        mesh=grid,
        in_specs=in_specs,
        out_specs=out_specs,
        check_vma=False,
    )
```

```python
import functools

import jax
import jax.numpy as jnp
from jax import lax
from jax.experimental import pallas as pl
from jax.experimental.pallas import tpu as pltpu
from jax.sharding import Mesh
from jax.sharding import PartitionSpec as P

LEARN_RATE = 0.5
ADAGRAD_EPS = 1e-08
REP = ("x", "core")
MIB = 1 << 20


def mask_kernel(n_z, count_ref, grad_ref, out_ref):
    tables, samples, width = out_ref.shape
    n_y = tables // n_z
    first = pl.program_id(0) * samples
    to = lax.broadcasted_iota(jnp.int32, (256, 256), 0)
    source = lax.broadcasted_iota(jnp.int32, (256, 256), 1)
    permute = ((source % 16) * 16 + source // 16 == to).astype(jnp.bfloat16)
    position = lax.broadcasted_iota(jnp.int32, (16, width), 0) + first
    for sample in range(0, samples, 16):
        for table in range(0, tables, 16):
            rows = grad_ref[sample : sample + 16, table : table + 16, :].reshape(256, width)
            moved = jnp.dot(permute, rows.astype(jnp.bfloat16), preferred_element_type=jnp.float32)
            for j in range(16):
                present = position + sample < count_ref[0, table + j]
                kept = jnp.where(present, moved[j * 16 : j * 16 + 16], 0.0)
                place = (table + j) % n_z * n_y + (table + j) // n_z
                out_ref[place, sample : sample + 16, :] = kept.astype(jnp.bfloat16)


def masked_by_table(n_z, pooled_grad, present_count):
    batch, tables, width = pooled_grad.shape
    samples = 128
    return pl.pallas_call(
        functools.partial(mask_kernel, n_z),
        grid=(batch // samples,),
        out_shape=jax.ShapeDtypeStruct((tables, batch, width), jnp.bfloat16),
        in_specs=[
            pl.BlockSpec(memory_space=pltpu.SMEM),
            pl.BlockSpec((samples, tables, width), lambda i: (i, 0, 0)),
        ],
        out_specs=pl.BlockSpec((tables, samples, width), lambda i: (0, i, 0)),
        compiler_params=pltpu.CompilerParams(vmem_limit_bytes=56 * MIB),
        cost_estimate=pl.CostEstimate(flops=batch * tables * width, bytes_accessed=batch * tables * width * 6, transcendentals=0),
        name="mask",
    )(present_count, pooled_grad)


def place_kernel(z_ref, members_ref, pos_ref, out_ref):
    n_z, slots, wide = out_ref.shape
    n_y = wide // 256
    parts = [jnp.broadcast_to(pos_ref[:, pl.ds(128 * k, 128)], (slots, 128)) for k in range(pos_ref.shape[1] // 128)]
    for j in range(n_z):
        z = lax.bitwise_xor(z_ref[0], j)
        for y in range(n_y):
            for half in range(2):
                start = pl.multiple_of((y * n_z + z) * 256 + half * 128, 128)
                member = members_ref[:, pl.ds(start, 128)]
                low, high = member & 127, member >> 7
                found = jnp.take_along_axis(parts[0], low, axis=1)
                for k in range(1, len(parts)):
                    found = jnp.where(high == k, jnp.take_along_axis(parts[k], low, axis=1), found)
                out_ref[j, :, pl.ds(y * 256 + half * 128, 128)] = found


def places_of(members, rep_pos, z, n_z):
    batch, slots = members.shape
    return pl.pallas_call(
        place_kernel,
        out_shape=jax.ShapeDtypeStruct((n_z, slots, batch // n_z), jnp.int32),
        in_specs=[
            pl.BlockSpec(memory_space=pltpu.SMEM),
            pl.BlockSpec(memory_space=pltpu.VMEM),
            pl.BlockSpec(memory_space=pltpu.VMEM),
        ],
        compiler_params=pltpu.CompilerParams(vmem_limit_bytes=8 * MIB),
        cost_estimate=pl.CostEstimate(flops=batch * slots * 8, bytes_accessed=batch * slots * 8, transcendentals=0),
        name="places",
    )(z, members.T, rep_pos)


def state_kernel(ids_ref, accum_ref, out_ref):
    low, high = ids_ref[...] & 127, ids_ref[...] >> 7
    found = jnp.zeros(out_ref.shape, jnp.float32)
    for k in range(accum_ref.shape[0]):
        row = jnp.broadcast_to(accum_ref[k : k + 1, :], out_ref.shape)
        found = jnp.where(high == k, jnp.take_along_axis(row, low, axis=1), found)
    out_ref[...] = found


def state_of(accum, row_ids):
    ids = row_ids.reshape(-1, 128)
    return pl.pallas_call(
        state_kernel,
        out_shape=jax.ShapeDtypeStruct(ids.shape, jnp.float32),
        compiler_params=pltpu.CompilerParams(vmem_limit_bytes=4 * MIB),
        cost_estimate=pl.CostEstimate(flops=accum.size * 8, bytes_accessed=accum.size * 4, transcendentals=0),
        name="state",
    )(ids, accum.reshape(-1, 128)).reshape(-1)


def turn(v):
    return (v ^ ((v & 1) * 11)) >> 1


def from_turn(v):
    return (v * 2) ^ (v // 4 * 11)


def exchange_over_z(places):
    n_z = places.shape[0]
    places = places.reshape((2, 2, 2) + places.shape[1:])
    for axis, bit in enumerate((4, 2, 1)):
        stay = lax.index_in_dim(places, 0, axis, False)
        go = lax.index_in_dim(places, 1, axis, False)
        come = lax.ppermute(go, "z", [(z, z ^ bit) for z in range(n_z)])
        places = jnp.stack([stay, come], axis)
    return places.reshape((n_z,) + places.shape[3:])


def sum_over_z(even, up, down, across, n_z):
    def shift(array, by):
        return lax.ppermute(array, "z", [(a, (a + by) % n_z) for a in range(n_z)])

    def plus(a, b):
        return a.astype(jnp.float32) + b.astype(jnp.float32)

    up, down, across = shift(up, 1), shift(down, -1), shift(across, 4)
    two_up = shift(plus(even[1], up[1]).astype(jnp.bfloat16), 2)
    two_down = shift(plus(even[2], down[0]).astype(jnp.bfloat16), -2)
    total = plus(even[0], up[0]) + plus(across, down[1]) + plus(two_up, two_down)
    return total.astype(jnp.bfloat16)


def gather_over_rep(part, n_x):
    x = lax.axis_index("x")
    place = (lax.broadcasted_iota(jnp.int32, (n_x, 1, 1), 0) - x + n_x) % n_x
    rows = part[None]
    for step in range(1, n_x):
        come = lax.ppermute(part, "x", [(a, (a - step) % n_x) for a in range(n_x)])
        rows = jnp.where(place == step, come[None], rows)
    return lax.all_gather(rows, "core", axis=1, tiled=False).reshape(-1, part.shape[1])


def one_hot_rows(values, row):
    return jnp.where(jnp.broadcast_to(values, row.shape) == row, jnp.bfloat16(1), jnp.bfloat16(0))


def count_kernel(place_ref, out_ref):
    slots, samples = place_ref.shape[1:]
    rows = 32
    base = lax.broadcasted_iota(jnp.int32, (rows, 128), 0).astype(jnp.bfloat16)

    def lanes(i, carry):
        at = pl.ds(pl.multiple_of(i * 128, 128), 128)
        place = place_ref[0, :, at]
        high, low = place >> 8, place & 255
        for block in range(out_ref.shape[1] // 256):
            wanted = jnp.where(high == block, low, -1).astype(jnp.bfloat16)
            for first in range(0, 256, rows):
                row = base + jnp.bfloat16(first)
                total = one_hot_rows(wanted[0:1], row)
                for s in range(1, slots):
                    total = total + one_hot_rows(wanted[s : s + 1], row)
                out_ref[0, pl.ds(block * 256 + first, rows), at] = total.astype(out_ref.dtype)
        return carry

    lax.fori_loop(0, samples // 128, lanes, 0)


def counts_of(places, active):
    reps, slots, wide = places.shape
    return pl.pallas_call(
        count_kernel,
        grid=(reps,),
        in_specs=[pl.BlockSpec((1, slots, wide), lambda j: (j, 0, 0))],
        out_specs=pl.BlockSpec((1, active, wide), lambda j: (j, 0, 0)),
        out_shape=jax.ShapeDtypeStruct((reps, active, wide), jnp.float8_e4m3fn),
        compiler_params=pltpu.CompilerParams(vmem_limit_bytes=56 * MIB),
        cost_estimate=pl.CostEstimate(flops=active * wide * reps * slots * 3, bytes_accessed=active * wide * reps, transcendentals=0),
        name="counts",
    )(places)


AHEAD = 4


def plane_kernel(z_ref, rep_ref, count_hbm, bags_hbm, even_ref, up_ref, down_ref, across_ref, count_buf, bags_buf, total_ref, count_sem, bags_sem):
    reps, _, samples = count_hbm.shape
    n_z, rows = 8, across_ref.shape[0]

    def copies(j):
        slot = lax.rem(j, AHEAD)
        group = rep_ref[0] ^ from_turn(z_ref[0] ^ j ^ rep_ref[0])
        start = pl.multiple_of(group * samples, samples)
        return (
            pltpu.make_async_copy(count_hbm.at[j], count_buf.at[slot], count_sem.at[slot]),
            pltpu.make_async_copy(bags_hbm.at[pl.ds(start, samples), :], bags_buf.at[slot], bags_sem.at[slot]),
        )

    for j in range(AHEAD - 1):
        for copy in copies(jnp.int32(j)):
            copy.start()
    total_ref[...] = jnp.zeros_like(total_ref)

    def step(j, carry):
        @pl.when(j + AHEAD - 1 < reps)
        def _():
            for copy in copies(j + AHEAD - 1):
                copy.start()

        for copy in copies(j):
            copy.wait()
        slot = lax.rem(j, AHEAD)
        counts = count_buf[slot].astype(jnp.bfloat16)
        total_ref[...] += jnp.dot(counts, bags_buf[slot], preferred_element_type=jnp.float32)
        return carry

    lax.fori_loop(0, reps, step, 0)
    def rows_for(k):
        first = pl.multiple_of(lax.rem(z_ref[0] + k, n_z) * rows, rows)
        return total_ref[pl.ds(first, rows), :].astype(jnp.bfloat16)

    for out_ref, ks in ((even_ref, (0, 2, 6)), (up_ref, (1, 3)), (down_ref, (5, 7))):
        for place, k in enumerate(ks):
            out_ref[place] = rows_for(k)
    across_ref[...] = rows_for(4)


def plane_sum(z, rep, counts, bags, n_z):
    reps, active, samples = counts.shape
    width = bags.shape[1]
    return pl.pallas_call(
        plane_kernel,
        out_shape=[jax.ShapeDtypeStruct(lead + (active // n_z, width), jnp.bfloat16) for lead in ((3,), (2,), (2,), ())],
        in_specs=[
            pl.BlockSpec(memory_space=pltpu.SMEM),
            pl.BlockSpec(memory_space=pltpu.SMEM),
            pl.BlockSpec(memory_space=pl.ANY),
            pl.BlockSpec(memory_space=pl.ANY),
        ],
        out_specs=[pl.BlockSpec(memory_space=pltpu.VMEM)] * 4,
        scratch_shapes=[
            pltpu.VMEM((AHEAD, active, samples), counts.dtype),
            pltpu.VMEM((AHEAD, samples, width), jnp.bfloat16),
            pltpu.VMEM((active, width), jnp.float32),
            pltpu.SemaphoreType.DMA((AHEAD,)),
            pltpu.SemaphoreType.DMA((AHEAD,)),
        ],
        compiler_params=pltpu.CompilerParams(vmem_limit_bytes=56 * MIB),
        cost_estimate=pl.CostEstimate(
            flops=2 * reps * active * samples * width,
            bytes_accessed=reps * samples * (active + 2 * width),
            transcendentals=0,
        ),
        name="plane_sum",
    )(z, rep, counts, bags)


def local(n_z, n_rep, pooled_grad, present_count, members, rep_pos, row_ids, table, accum):
    active, width = row_ids.shape[1], pooled_grad.shape[2]
    swap = [(z * n_rep + q, q * n_z + z) for z in range(n_z) for q in range(n_rep)]

    z, rep = lax.axis_index("z"), lax.axis_index(REP)
    spread = [(a * n_rep + r, (a ^ turn(r ^ a)) * n_rep + a) for a in range(n_z) for r in range(n_rep)]
    plane = z ^ turn(z ^ rep)
    places = places_of(members[:, 0, :], rep_pos[0], plane.reshape(1), n_z).astype(jnp.int16)
    places = lax.ppermute(places, ("z",) + REP, spread)
    places = exchange_over_z(places)
    old_rows = jnp.take(table[0], row_ids[0], axis=0)
    old_state = state_of(accum[0], row_ids[0])
    places, old_rows, old_state = lax.optimization_barrier((places, old_rows, old_state))
    places = places.astype(jnp.int32)

    masked = masked_by_table(n_z, pooled_grad, present_count)
    arrived = lax.all_to_all(masked, REP + ("y",), split_axis=0, concat_axis=0, tiled=True)

    counts = counts_of(places, active)
    partial = plane_sum(z.reshape(1), rep.reshape(1), counts, arrived.reshape(-1, width), n_z)

    part = sum_over_z(*partial, n_z)
    part = lax.ppermute(part, ("z",) + REP, swap)
    summed = gather_over_rep(part, n_rep // 2).astype(jnp.float32)

    new_state = old_state + jnp.mean(summed * summed, axis=1)
    updated = old_rows - LEARN_RATE * summed / (jnp.sqrt(new_state)[:, None] + ADAGRAD_EPS)
    return (updated[None], new_state[None])


def solution(mesh):
    n_y, n_z, n_x, n_core = 4, 8, 4, 2
    grid = Mesh(mesh.devices.reshape(n_y, n_z, n_x, n_core), ("y", "z", "x", "core"))
    shard = ("y", "z")
    in_specs = (
        P(REP + shard, None, None),
        P(REP + shard, None),
        P(REP, shard, None),
        P(REP, shard, None),
        P(shard, None),
        P(shard, None, None),
        P(shard, None),
    )
    out_specs = (P(shard, None, None), P(shard, None))
    return jax.shard_map(
        functools.partial(local, n_z, n_x * n_core),
        mesh=grid,
        in_specs=in_specs,
        out_specs=out_specs,
        check_vma=False,
    )
```

```python
import functools

import jax
import jax.numpy as jnp
from jax import lax
from jax.experimental import pallas as pl
from jax.experimental.pallas import tpu as pltpu
from jax.sharding import Mesh
from jax.sharding import PartitionSpec as P

LEARN_RATE = 0.5
ADAGRAD_EPS = 1e-08
REP = ("x", "core")
MIB = 1 << 20


def mask_kernel(n_z, count_ref, grad_ref, out_ref):
    tables, samples, width = out_ref.shape
    n_y = tables // n_z
    first = pl.program_id(0) * samples
    to = lax.broadcasted_iota(jnp.int32, (256, 256), 0)
    source = lax.broadcasted_iota(jnp.int32, (256, 256), 1)
    permute = ((source % 16) * 16 + source // 16 == to).astype(jnp.bfloat16)
    position = lax.broadcasted_iota(jnp.int32, (16, width), 0) + first
    for sample in range(0, samples, 16):
        for table in range(0, tables, 16):
            rows = grad_ref[sample : sample + 16, table : table + 16, :].reshape(256, width)
            moved = jnp.dot(permute, rows.astype(jnp.bfloat16), preferred_element_type=jnp.float32)
            for j in range(16):
                present = position + sample < count_ref[0, table + j]
                kept = jnp.where(present, moved[j * 16 : j * 16 + 16], 0.0)
                place = (table + j) % n_z * n_y + (table + j) // n_z
                out_ref[place, sample : sample + 16, :] = kept.astype(jnp.bfloat16)


def masked_by_table(n_z, pooled_grad, present_count):
    batch, tables, width = pooled_grad.shape
    samples = 128
    return pl.pallas_call(
        functools.partial(mask_kernel, n_z),
        grid=(batch // samples,),
        out_shape=jax.ShapeDtypeStruct((tables, batch, width), jnp.bfloat16),
        in_specs=[
            pl.BlockSpec(memory_space=pltpu.SMEM),
            pl.BlockSpec((samples, tables, width), lambda i: (i, 0, 0)),
        ],
        out_specs=pl.BlockSpec((tables, samples, width), lambda i: (0, i, 0)),
        compiler_params=pltpu.CompilerParams(vmem_limit_bytes=56 * MIB),
        cost_estimate=pl.CostEstimate(flops=batch * tables * width, bytes_accessed=batch * tables * width * 6, transcendentals=0),
        name="mask",
    )(present_count, pooled_grad)


def place_kernel(z_ref, members_ref, pos_ref, out_ref):
    n_z, slots, wide = out_ref.shape
    n_y = wide // 256
    parts = [jnp.broadcast_to(pos_ref[:, pl.ds(128 * k, 128)], (slots, 128)) for k in range(pos_ref.shape[1] // 128)]
    for j in range(n_z):
        z = lax.bitwise_xor(z_ref[0], j)
        for y in range(n_y):
            for half in range(2):
                start = pl.multiple_of((y * n_z + z) * 256 + half * 128, 128)
                member = members_ref[:, pl.ds(start, 128)]
                low, high = member & 127, member >> 7
                found = jnp.take_along_axis(parts[0], low, axis=1)
                for k in range(1, len(parts)):
                    found = jnp.where(high == k, jnp.take_along_axis(parts[k], low, axis=1), found)
                out_ref[j, :, pl.ds(y * 256 + half * 128, 128)] = found


def places_of(members, rep_pos, z, n_z):
    batch, slots = members.shape
    return pl.pallas_call(
        place_kernel,
        out_shape=jax.ShapeDtypeStruct((n_z, slots, batch // n_z), jnp.int32),
        in_specs=[
            pl.BlockSpec(memory_space=pltpu.SMEM),
            pl.BlockSpec(memory_space=pltpu.VMEM),
            pl.BlockSpec(memory_space=pltpu.VMEM),
        ],
        compiler_params=pltpu.CompilerParams(vmem_limit_bytes=8 * MIB),
        cost_estimate=pl.CostEstimate(flops=batch * slots * 8, bytes_accessed=batch * slots * 8, transcendentals=0),
        name="places",
    )(z, members.T, rep_pos)


def state_kernel(ids_ref, accum_ref, out_ref):
    low, high = ids_ref[...] & 127, ids_ref[...] >> 7
    found = jnp.zeros(out_ref.shape, jnp.float32)
    for k in range(accum_ref.shape[0]):
        row = jnp.broadcast_to(accum_ref[k : k + 1, :], out_ref.shape)
        found = jnp.where(high == k, jnp.take_along_axis(row, low, axis=1), found)
    out_ref[...] = found


def state_of(accum, row_ids):
    ids = row_ids.reshape(-1, 128)
    return pl.pallas_call(
        state_kernel,
        out_shape=jax.ShapeDtypeStruct(ids.shape, jnp.float32),
        compiler_params=pltpu.CompilerParams(vmem_limit_bytes=4 * MIB),
        cost_estimate=pl.CostEstimate(flops=accum.size * 8, bytes_accessed=accum.size * 4, transcendentals=0),
        name="state",
    )(ids, accum.reshape(-1, 128)).reshape(-1)


def turn(v):
    return (v ^ ((v & 1) * 11)) >> 1


def from_turn(v):
    return (v * 2) ^ (v // 4 * 11)


def exchange_over_z(places):
    n_z = places.shape[0]
    places = places.reshape((2, 2, 2) + places.shape[1:])
    for axis, bit in enumerate((4, 2, 1)):
        stay = lax.index_in_dim(places, 0, axis, False)
        go = lax.index_in_dim(places, 1, axis, False)
        come = lax.ppermute(go, "z", [(z, z ^ bit) for z in range(n_z)])
        places = jnp.stack([stay, come], axis)
    return places.reshape((n_z,) + places.shape[3:])


def sum_over_z(even, up, down, across, n_z):
    def shift(array, by):
        return lax.ppermute(array, "z", [(a, (a + by) % n_z) for a in range(n_z)])

    def plus(a, b):
        return a.astype(jnp.float32) + b.astype(jnp.float32)

    up, down, across = shift(up, 1), shift(down, -1), shift(across, 4)
    two_up = shift(plus(even[1], up[1]).astype(jnp.bfloat16), 2)
    two_down = shift(plus(even[2], down[0]).astype(jnp.bfloat16), -2)
    total = plus(even[0], up[0]) + plus(across, down[1]) + plus(two_up, two_down)
    return total.astype(jnp.bfloat16)


def gather_over_rep(part, n_x):
    x = lax.axis_index("x")
    place = (lax.broadcasted_iota(jnp.int32, (n_x, 1, 1), 0) - x + n_x) % n_x
    rows = part[None]
    for step in range(1, n_x):
        come = lax.ppermute(part, "x", [(a, (a - step) % n_x) for a in range(n_x)])
        rows = jnp.where(place == step, come[None], rows)
    return lax.all_gather(rows, "core", axis=1, tiled=False).reshape(-1, part.shape[1])


def one_hot_rows(values, row):
    return jnp.where(jnp.broadcast_to(values, row.shape) == row, jnp.bfloat16(1), jnp.bfloat16(0))


def count_kernel(place_ref, out_ref):
    slots, samples = place_ref.shape[1:]
    rows = 32
    base = lax.broadcasted_iota(jnp.int32, (rows, 128), 0).astype(jnp.bfloat16)

    def lanes(i, carry):
        at = pl.ds(pl.multiple_of(i * 128, 128), 128)
        place = place_ref[0, :, at]
        high, low = place >> 8, place & 255
        for block in range(out_ref.shape[1] // 256):
            wanted = jnp.where(high == block, low, -1).astype(jnp.bfloat16)
            for first in range(0, 256, rows):
                row = base + jnp.bfloat16(first)
                total = one_hot_rows(wanted[0:1], row)
                for s in range(1, slots):
                    total = total + one_hot_rows(wanted[s : s + 1], row)
                out_ref[0, pl.ds(block * 256 + first, rows), at] = total.astype(out_ref.dtype)
        return carry

    lax.fori_loop(0, samples // 128, lanes, 0)


def counts_of(places, active, first, dtype):
    reps, slots, wide = places.shape
    reps = reps // 2
    return pl.pallas_call(
        count_kernel,
        grid=(reps,),
        in_specs=[pl.BlockSpec((1, slots, wide), lambda j: (first + j, 0, 0))],
        out_specs=pl.BlockSpec((1, active, wide), lambda j: (j, 0, 0)),
        out_shape=jax.ShapeDtypeStruct((reps, active, wide), dtype),
        compiler_params=pltpu.CompilerParams(vmem_limit_bytes=56 * MIB),
        cost_estimate=pl.CostEstimate(flops=active * wide * reps * slots * 3, bytes_accessed=active * wide * reps, transcendentals=0),
        name="counts",
    )(places)


AHEAD = 3


def plane_kernel(z_ref, rep_ref, small_hbm, large_hbm, bags_hbm, even_ref, up_ref, down_ref, across_ref, *scratch):
    small_buf, large_buf, small_bags, large_bags, total_ref, sems = scratch
    steps, _, samples = small_hbm.shape
    n_z, rows = 8, across_ref.shape[0]

    def copies(i):
        slot = lax.rem(i, AHEAD)
        found = []
        for part, (count_hbm, count_buf, bags_buf) in enumerate(
            ((small_hbm, small_buf, small_bags), (large_hbm, large_buf, large_bags))
        ):
            group = rep_ref[0] ^ from_turn(z_ref[0] ^ (i + part * steps) ^ rep_ref[0])
            bags = bags_hbm.at[pl.ds(pl.multiple_of(group * samples, samples), samples), :]
            found.append(pltpu.make_async_copy(count_hbm.at[i], count_buf.at[slot], sems.at[2 * part, slot]))
            found.append(pltpu.make_async_copy(bags, bags_buf.at[slot], sems.at[2 * part + 1, slot]))
        return found

    for i in range(AHEAD - 1):
        for copy in copies(jnp.int32(i)):
            copy.start()
    total_ref[...] = jnp.zeros_like(total_ref)

    def step(i, carry):
        @pl.when(i + AHEAD - 1 < steps)
        def _():
            for copy in copies(i + AHEAD - 1):
                copy.start()

        for copy in copies(i):
            copy.wait()
        slot = lax.rem(i, AHEAD)
        small = small_buf[slot].astype(jnp.bfloat16)
        sums = jnp.dot(small, small_bags[slot], preferred_element_type=jnp.float32)
        sums += jnp.dot(large_buf[slot], large_bags[slot], preferred_element_type=jnp.float32)
        total_ref[...] += sums
        return carry

    lax.fori_loop(0, steps, step, 0)

    def rows_for(k):
        first = pl.multiple_of(lax.rem(z_ref[0] + k, n_z) * rows, rows)
        return total_ref[pl.ds(first, rows), :].astype(jnp.bfloat16)

    for out_ref, ks in ((even_ref, (0, 2, 6)), (up_ref, (1, 3)), (down_ref, (5, 7))):
        for place, k in enumerate(ks):
            out_ref[place] = rows_for(k)
    across_ref[...] = rows_for(4)


def plane_sum(z, rep, small, large, bags, n_z):
    steps, active, samples = small.shape
    width = bags.shape[1]
    return pl.pallas_call(
        plane_kernel,
        out_shape=[jax.ShapeDtypeStruct(lead + (active // n_z, width), jnp.bfloat16) for lead in ((3,), (2,), (2,), ())],
        in_specs=[pl.BlockSpec(memory_space=pltpu.SMEM)] * 2 + [pl.BlockSpec(memory_space=pl.ANY)] * 3,
        out_specs=[pl.BlockSpec(memory_space=pltpu.VMEM)] * 4,
        scratch_shapes=[
            pltpu.VMEM((AHEAD, active, samples), small.dtype),
            pltpu.VMEM((AHEAD, active, samples), large.dtype),
            pltpu.VMEM((AHEAD, samples, width), jnp.bfloat16),
            pltpu.VMEM((AHEAD, samples, width), jnp.bfloat16),
            pltpu.VMEM((active, width), jnp.float32),
            pltpu.SemaphoreType.DMA((4, AHEAD)),
        ],
        compiler_params=pltpu.CompilerParams(vmem_limit_bytes=56 * MIB),
        cost_estimate=pl.CostEstimate(
            flops=4 * steps * active * samples * width,
            bytes_accessed=steps * samples * (3 * active + 4 * width),
            transcendentals=0,
        ),
        name="plane_sum",
    )(z, rep, small, large, bags)


def local(n_z, n_rep, pooled_grad, present_count, members, rep_pos, row_ids, table, accum):
    active, width = row_ids.shape[1], pooled_grad.shape[2]
    swap = [(z * n_rep + q, q * n_z + z) for z in range(n_z) for q in range(n_rep)]

    z, rep = lax.axis_index("z"), lax.axis_index(REP)
    spread = [(a * n_rep + r, (a ^ turn(r ^ a)) * n_rep + a) for a in range(n_z) for r in range(n_rep)]
    plane = z ^ turn(z ^ rep)
    places = places_of(members[:, 0, :], rep_pos[0], plane.reshape(1), n_z).astype(jnp.int16)
    places = lax.ppermute(places, ("z",) + REP, spread)
    places = exchange_over_z(places)
    old_rows = jnp.take(table[0], row_ids[0], axis=0)
    old_state = state_of(accum[0], row_ids[0])
    places, old_rows, old_state = lax.optimization_barrier((places, old_rows, old_state))
    places = places.astype(jnp.int32)

    masked = masked_by_table(n_z, pooled_grad, present_count)
    arrived = lax.all_to_all(masked, REP + ("y",), split_axis=0, concat_axis=0, tiled=True)

    small = counts_of(places, active, 0, jnp.float8_e4m3fn)
    large = counts_of(places, active, n_z // 2, jnp.bfloat16)
    partial = plane_sum(z.reshape(1), rep.reshape(1), small, large, arrived.reshape(-1, width), n_z)

    part = sum_over_z(*partial, n_z)
    part = lax.ppermute(part, ("z",) + REP, swap)
    summed = gather_over_rep(part, n_rep // 2).astype(jnp.float32)

    new_state = old_state + jnp.mean(summed * summed, axis=1)
    updated = old_rows - LEARN_RATE * summed / (jnp.sqrt(new_state)[:, None] + ADAGRAD_EPS)
    return (updated[None], new_state[None])


def solution(mesh):
    n_y, n_z, n_x, n_core = 4, 8, 4, 2
    grid = Mesh(mesh.devices.reshape(n_y, n_z, n_x, n_core), ("y", "z", "x", "core"))
    shard = ("y", "z")
    in_specs = (
        P(REP + shard, None, None),
        P(REP + shard, None),
        P(REP, shard, None),
        P(REP, shard, None),
        P(shard, None),
        P(shard, None, None),
        P(shard, None),
    )
    out_specs = (P(shard, None, None), P(shard, None))
    return jax.shard_map(
        functools.partial(local, n_z, n_x * n_core),
        mesh=grid,
        in_specs=in_specs,
        out_specs=out_specs,
        check_vma=False,
    )
```

```python
import functools

import jax
import jax.numpy as jnp
from jax import lax
from jax.experimental import pallas as pl
from jax.experimental.pallas import tpu as pltpu
from jax.sharding import Mesh
from jax.sharding import PartitionSpec as P

LEARN_RATE = 0.5
ADAGRAD_EPS = 1e-08
REP = ("x", "core")
MIB = 1 << 20


def mask_kernel(n_z, count_ref, grad_ref, out_ref):
    tables, samples, width = out_ref.shape
    n_y = tables // n_z
    first = pl.program_id(0) * samples
    to = lax.broadcasted_iota(jnp.int32, (256, 256), 0)
    source = lax.broadcasted_iota(jnp.int32, (256, 256), 1)
    permute = ((source % 16) * 16 + source // 16 == to).astype(jnp.bfloat16)
    position = lax.broadcasted_iota(jnp.int32, (16, width), 0) + first
    for sample in range(0, samples, 16):
        for table in range(0, tables, 16):
            rows = grad_ref[sample : sample + 16, table : table + 16, :].reshape(256, width)
            moved = jnp.dot(permute, rows.astype(jnp.bfloat16), preferred_element_type=jnp.float32)
            for j in range(16):
                present = position + sample < count_ref[0, table + j]
                kept = jnp.where(present, moved[j * 16 : j * 16 + 16], 0.0)
                place = (table + j) % n_z * n_y + (table + j) // n_z
                out_ref[place, sample : sample + 16, :] = kept.astype(jnp.bfloat16)


def masked_by_table(n_z, pooled_grad, present_count):
    batch, tables, width = pooled_grad.shape
    samples = 128
    return pl.pallas_call(
        functools.partial(mask_kernel, n_z),
        grid=(batch // samples,),
        out_shape=jax.ShapeDtypeStruct((tables, batch, width), jnp.bfloat16),
        in_specs=[
            pl.BlockSpec(memory_space=pltpu.SMEM),
            pl.BlockSpec((samples, tables, width), lambda i: (i, 0, 0)),
        ],
        out_specs=pl.BlockSpec((tables, samples, width), lambda i: (0, i, 0)),
        compiler_params=pltpu.CompilerParams(vmem_limit_bytes=56 * MIB),
        cost_estimate=pl.CostEstimate(flops=batch * tables * width, bytes_accessed=batch * tables * width * 6, transcendentals=0),
        name="mask",
    )(present_count, pooled_grad)


def place_kernel(z_ref, members_ref, pos_ref, out_ref):
    n_z, slots, wide = out_ref.shape
    n_y = wide // 256
    parts = [jnp.broadcast_to(pos_ref[:, pl.ds(128 * k, 128)], (slots, 128)) for k in range(pos_ref.shape[1] // 128)]
    for j in range(n_z):
        z = lax.bitwise_xor(z_ref[0], j)
        for y in range(n_y):
            for half in range(2):
                start = pl.multiple_of((y * n_z + z) * 256 + half * 128, 128)
                member = members_ref[:, pl.ds(start, 128)]
                low, high = member & 127, member >> 7
                found = jnp.take_along_axis(parts[0], low, axis=1)
                for k in range(1, len(parts)):
                    found = jnp.where(high == k, jnp.take_along_axis(parts[k], low, axis=1), found)
                out_ref[j, :, pl.ds(y * 256 + half * 128, 128)] = found


def places_of(members, rep_pos, z, n_z):
    batch, slots = members.shape
    return pl.pallas_call(
        place_kernel,
        out_shape=jax.ShapeDtypeStruct((n_z, slots, batch // n_z), jnp.int32),
        in_specs=[
            pl.BlockSpec(memory_space=pltpu.SMEM),
            pl.BlockSpec(memory_space=pltpu.VMEM),
            pl.BlockSpec(memory_space=pltpu.VMEM),
        ],
        compiler_params=pltpu.CompilerParams(vmem_limit_bytes=8 * MIB),
        cost_estimate=pl.CostEstimate(flops=batch * slots * 8, bytes_accessed=batch * slots * 8, transcendentals=0),
        name="places",
    )(z, members.T, rep_pos)


def state_kernel(ids_ref, accum_ref, out_ref):
    low, high = ids_ref[...] & 127, ids_ref[...] >> 7
    found = jnp.zeros(out_ref.shape, jnp.float32)
    for k in range(accum_ref.shape[0]):
        row = jnp.broadcast_to(accum_ref[k : k + 1, :], out_ref.shape)
        found = jnp.where(high == k, jnp.take_along_axis(row, low, axis=1), found)
    out_ref[...] = found


def state_of(accum, row_ids):
    ids = row_ids.reshape(-1, 128)
    return pl.pallas_call(
        state_kernel,
        out_shape=jax.ShapeDtypeStruct(ids.shape, jnp.float32),
        compiler_params=pltpu.CompilerParams(vmem_limit_bytes=4 * MIB),
        cost_estimate=pl.CostEstimate(flops=accum.size * 8, bytes_accessed=accum.size * 4, transcendentals=0),
        name="state",
    )(ids, accum.reshape(-1, 128)).reshape(-1)


def turn(v):
    return (v ^ ((v & 1) * 11)) >> 1


def from_turn(v):
    return (v * 2) ^ (v // 4 * 11)


def exchange_over_z(places):
    n_z = places.shape[0]
    places = places.reshape((2, 2, 2) + places.shape[1:])
    for axis, bit in enumerate((4, 2, 1)):
        stay = lax.index_in_dim(places, 0, axis, False)
        go = lax.index_in_dim(places, 1, axis, False)
        come = lax.ppermute(go, "z", [(z, z ^ bit) for z in range(n_z)])
        places = jnp.stack([stay, come], axis)
    return places.reshape((n_z,) + places.shape[3:])


def sum_over_z(even, up, down, across, n_z):
    def shift(array, by):
        return lax.ppermute(array, "z", [(a, (a + by) % n_z) for a in range(n_z)])

    def plus(a, b):
        return a.astype(jnp.float32) + b.astype(jnp.float32)

    up, down = shift(up, 1), shift(down, -1)
    two_up, two_down = plus(even[1], up[1]).astype(jnp.bfloat16), plus(even[2], down[0]).astype(jnp.bfloat16)
    two_up, two_down, across = lax.optimization_barrier((two_up, two_down, across))
    two_up, two_down, across = shift(two_up, 2), shift(two_down, -2), shift(across, 4)
    total = plus(even[0], up[0]) + plus(across, down[1]) + plus(two_up, two_down)
    return total.astype(jnp.bfloat16)


def gather_over_rep(part, n_x):
    x = lax.axis_index("x")
    place = (lax.broadcasted_iota(jnp.int32, (n_x, 1, 1), 0) - x + n_x) % n_x
    rows = part[None]
    for step in range(1, n_x):
        come = lax.ppermute(part, "x", [(a, (a - step) % n_x) for a in range(n_x)])
        rows = jnp.where(place == step, come[None], rows)
    return lax.all_gather(rows, "core", axis=1, tiled=False).reshape(-1, part.shape[1])


def one_hot_rows(values, row):
    return jnp.where(jnp.broadcast_to(values, row.shape) == row, jnp.bfloat16(1), jnp.bfloat16(0))


def count_kernel(place_ref, out_ref):
    slots, samples = place_ref.shape[1:]
    rows = 32
    base = lax.broadcasted_iota(jnp.int32, (rows, 128), 0).astype(jnp.bfloat16)

    def lanes(i, carry):
        at = pl.ds(pl.multiple_of(i * 128, 128), 128)
        place = place_ref[0, :, at]
        high, low = place >> 8, place & 255
        for block in range(out_ref.shape[1] // 256):
            wanted = jnp.where(high == block, low, -1).astype(jnp.bfloat16)
            for first in range(0, 256, rows):
                row = base + jnp.bfloat16(first)
                total = one_hot_rows(wanted[0:1], row)
                for s in range(1, slots):
                    total = total + one_hot_rows(wanted[s : s + 1], row)
                out_ref[0, pl.ds(block * 256 + first, rows), at] = total.astype(out_ref.dtype)
        return carry

    lax.fori_loop(0, samples // 128, lanes, 0)


def counts_of(places, active, first, dtype):
    reps, slots, wide = places.shape
    reps = reps // 2
    return pl.pallas_call(
        count_kernel,
        grid=(reps,),
        in_specs=[pl.BlockSpec((1, slots, wide), lambda j: (first + j, 0, 0))],
        out_specs=pl.BlockSpec((1, active, wide), lambda j: (j, 0, 0)),
        out_shape=jax.ShapeDtypeStruct((reps, active, wide), dtype),
        compiler_params=pltpu.CompilerParams(vmem_limit_bytes=56 * MIB),
        cost_estimate=pl.CostEstimate(flops=active * wide * reps * slots * 3, bytes_accessed=active * wide * reps, transcendentals=0),
        name="counts",
    )(places)


AHEAD = 3


def plane_kernel(z_ref, rep_ref, small_hbm, large_hbm, bags_hbm, even_ref, up_ref, down_ref, across_ref, *scratch):
    small_buf, large_buf, small_bags, large_bags, total_ref, sems = scratch
    steps, _, samples = small_hbm.shape
    n_z, rows = 8, across_ref.shape[0]

    def copies(i):
        slot = lax.rem(i, AHEAD)
        found = []
        for part, (count_hbm, count_buf, bags_buf) in enumerate(
            ((small_hbm, small_buf, small_bags), (large_hbm, large_buf, large_bags))
        ):
            group = rep_ref[0] ^ from_turn(z_ref[0] ^ (i + part * steps) ^ rep_ref[0])
            bags = bags_hbm.at[pl.ds(pl.multiple_of(group * samples, samples), samples), :]
            found.append(pltpu.make_async_copy(count_hbm.at[i], count_buf.at[slot], sems.at[2 * part, slot]))
            found.append(pltpu.make_async_copy(bags, bags_buf.at[slot], sems.at[2 * part + 1, slot]))
        return found

    for i in range(AHEAD - 1):
        for copy in copies(jnp.int32(i)):
            copy.start()
    total_ref[...] = jnp.zeros_like(total_ref)

    def step(i, carry):
        @pl.when(i + AHEAD - 1 < steps)
        def _():
            for copy in copies(i + AHEAD - 1):
                copy.start()

        for copy in copies(i):
            copy.wait()
        slot = lax.rem(i, AHEAD)
        small = small_buf[slot].astype(jnp.bfloat16)
        sums = jnp.dot(small, small_bags[slot], preferred_element_type=jnp.float32)
        sums += jnp.dot(large_buf[slot], large_bags[slot], preferred_element_type=jnp.float32)
        total_ref[...] += sums
        return carry

    lax.fori_loop(0, steps, step, 0)

    def rows_for(k):
        first = pl.multiple_of(lax.rem(z_ref[0] + k, n_z) * rows, rows)
        return total_ref[pl.ds(first, rows), :].astype(jnp.bfloat16)

    for out_ref, ks in ((even_ref, (0, 2, 6)), (up_ref, (1, 3)), (down_ref, (5, 7))):
        for place, k in enumerate(ks):
            out_ref[place] = rows_for(k)
    across_ref[...] = rows_for(4)


def plane_sum(z, rep, small, large, bags, n_z):
    steps, active, samples = small.shape
    width = bags.shape[1]
    return pl.pallas_call(
        plane_kernel,
        out_shape=[jax.ShapeDtypeStruct(lead + (active // n_z, width), jnp.bfloat16) for lead in ((3,), (2,), (2,), ())],
        in_specs=[pl.BlockSpec(memory_space=pltpu.SMEM)] * 2 + [pl.BlockSpec(memory_space=pl.ANY)] * 3,
        out_specs=[pl.BlockSpec(memory_space=pltpu.VMEM)] * 4,
        scratch_shapes=[
            pltpu.VMEM((AHEAD, active, samples), small.dtype),
            pltpu.VMEM((AHEAD, active, samples), large.dtype),
            pltpu.VMEM((AHEAD, samples, width), jnp.bfloat16),
            pltpu.VMEM((AHEAD, samples, width), jnp.bfloat16),
            pltpu.VMEM((active, width), jnp.float32),
            pltpu.SemaphoreType.DMA((4, AHEAD)),
        ],
        compiler_params=pltpu.CompilerParams(vmem_limit_bytes=56 * MIB),
        cost_estimate=pl.CostEstimate(
            flops=4 * steps * active * samples * width,
            bytes_accessed=steps * samples * (3 * active + 4 * width),
            transcendentals=0,
        ),
        name="plane_sum",
    )(z, rep, small, large, bags)


def local(n_z, n_rep, pooled_grad, present_count, members, rep_pos, row_ids, table, accum):
    active, width = row_ids.shape[1], pooled_grad.shape[2]
    swap = [(z * n_rep + q, q * n_z + z) for z in range(n_z) for q in range(n_rep)]

    z, rep = lax.axis_index("z"), lax.axis_index(REP)
    spread = [(a * n_rep + r, (a ^ turn(r ^ a)) * n_rep + a) for a in range(n_z) for r in range(n_rep)]
    plane = z ^ turn(z ^ rep)
    places = places_of(members[:, 0, :], rep_pos[0], plane.reshape(1), n_z).astype(jnp.int16)
    places = lax.ppermute(places, ("z",) + REP, spread)
    places = exchange_over_z(places)
    old_rows = jnp.take(table[0], row_ids[0], axis=0)
    old_state = state_of(accum[0], row_ids[0])
    places, old_rows, old_state = lax.optimization_barrier((places, old_rows, old_state))
    places = places.astype(jnp.int32)

    masked = masked_by_table(n_z, pooled_grad, present_count)
    arrived = lax.all_to_all(masked, REP + ("y",), split_axis=0, concat_axis=0, tiled=True)

    small = counts_of(places, active, 0, jnp.float8_e4m3fn)
    large = counts_of(places, active, n_z // 2, jnp.bfloat16)
    partial = plane_sum(z.reshape(1), rep.reshape(1), small, large, arrived.reshape(-1, width), n_z)

    part = sum_over_z(*partial, n_z)
    part = lax.ppermute(part, ("z",) + REP, swap)
    summed = gather_over_rep(part, n_rep // 2).astype(jnp.float32)

    new_state = old_state + jnp.mean(summed * summed, axis=1)
    updated = old_rows - LEARN_RATE * summed / (jnp.sqrt(new_state)[:, None] + ADAGRAD_EPS)
    return (updated[None], new_state[None])


def solution(mesh):
    n_y, n_z, n_x, n_core = 4, 8, 4, 2
    grid = Mesh(mesh.devices.reshape(n_y, n_z, n_x, n_core), ("y", "z", "x", "core"))
    shard = ("y", "z")
    in_specs = (
        P(REP + shard, None, None),
        P(REP + shard, None),
        P(REP, shard, None),
        P(REP, shard, None),
        P(shard, None),
        P(shard, None, None),
        P(shard, None),
    )
    out_specs = (P(shard, None, None), P(shard, None))
    return jax.shard_map(
        functools.partial(local, n_z, n_x * n_core),
        mesh=grid,
        in_specs=in_specs,
        out_specs=out_specs,
        check_vma=False,
    )
```
